32 devices in a mesh: azim: 4 (over y, x), axial: 4 (over z), pair: 2 (over core).
Axes of the slice: x: 2, y: 2, z: 4, core: 2. Of those that a mesh axis runs over, the one named last changes fastest.
Arguments:
- forcing: float32 [64, 160, 256], P('azim', 'axial', 'pair'), may hold values from -12 to 12
- absorption: float32 [64, 160, 256], P('azim', 'axial', 'pair'), may hold values from 0.02 to 2
- blocks: int32 [16, 40, 64], P('azim', 'axial', 'pair'), may hold values 0 or 1
Outputs:
- pressure: float32 [64, 160, 256], P('azim', 'axial', 'pair')
- residual: float32 [64, 160, 256], P('azim', 'axial', 'pair')
The draws below stay inside these ranges and needn't reach their ends.
All inputs are finite; a program needn't handle non-finite values. No bound on the sum of `blocks` on one device may be relied on, other than what follows from the above.
Results may differ from the reference program's by a relative error of at most 0.0003.
Values sent between devices are 32-bit elements; how exact they have to be, the bound alone decides.
A program may use at most 128 MiB of HBM per device.

```python
import math
import jax
import jax.numpy as jnp

LEVELS = 4
SWEEPS = 2
COARSE_SWEEPS = 4
CYCLES = 2
NA = 64
NX = 160
NR = 256


def plant(entries, key, low, largest):
    index_at = [jax.random.randint(jax.random.fold_in(key, axis), (), 0, length) for axis, length in enumerate(entries.shape)]
    longest = entries.shape.index(max(entries.shape))
    next_to = index_at[:longest] + [(index_at[longest] + 1) % entries.shape[longest]] + index_at[longest + 1:]
    return entries.at[tuple(index_at)].set(low).at[tuple(next_to)].set(largest)


def levels(own_key, dims, cuts, least, high):
    factor_of, own = 1.0, jax.random.fold_in(own_key, 6)
    for dim, parts in cuts:
        steps = jnp.exp(jax.random.uniform(jax.random.fold_in(own, dim), (parts,), jnp.float32, least / len(cuts), high / len(cuts)))
        factor_of = factor_of * jnp.repeat(steps, dims[dim] // parts).reshape([-1 if axis == dim else 1 for axis in range(len(dims))])
    return factor_of


def normal_values(own_key, shape, deviation, most, cuts=(), held_as=jnp.bfloat16):
    entries = jax.random.normal(own_key, shape, jnp.float32) * deviation
    if len(cuts) > 0:
        entries = levels(own_key, shape, cuts, -0.22, 0.18) * entries
    return jnp.clip(entries, min=-most, max=most).astype(held_as)


def setup_inputs(seed: int = 0) -> dict:
    keys = jax.random.split(jax.random.key(seed), 4)
    forcing = normal_values(keys[0], (NA, NX, NR), 2.0, 12.0, ((0, 4), (1, 4), (2, 2)), jnp.float32)
    absorption = jnp.clip(jnp.exp(math.log(2.0) - 4.6051702 * jax.random.uniform(keys[1], (NA, NX, NR), jnp.float32) ** levels(keys[1], (NA, NX, NR), ((0, 4), (1, 4), (2, 2)), -0.2, 0.2)), 0.02, 2.0)
    blocks = plant((jax.random.randint(keys[2], (NA // 4, NX // 4, NR // 4), 0, 4) < 3).astype(jnp.int32), jax.random.fold_in(keys[2], 1), 0, 1)
    return {"forcing": forcing, "absorption": absorption, "blocks": blocks}


DAMPING = 0.8


def expand(blocks):
    a, b, c = blocks.shape
    fluid = blocks.astype(jnp.float32)
    fluid = jnp.broadcast_to(fluid[:, None, :, None, :, None], (a, 4, b, 4, c, 4))
    return fluid.reshape(a * 4, b * 4, c * 4)


def coarsen(values, reducer):
    a, b, c = values.shape
    grouped = values.reshape(a // 2, 2, b // 2, 2, c // 2, 2)
    return reducer(grouped, axis=(1, 3, 5))


def refine(values):
    a, b, c = values.shape
    spread = jnp.broadcast_to(values[:, None, :, None, :, None], (a, 2, b, 2, c, 2))
    return spread.reshape(a * 2, b * 2, c * 2)


def face_sum(padded):
    total = padded[2:, 1:-1, 1:-1] + padded[:-2, 1:-1, 1:-1]
    total = total + padded[1:-1, 2:, 1:-1] + padded[1:-1, :-2, 1:-1]
    return total + padded[1:-1, 1:-1, 2:] + padded[1:-1, 1:-1, :-2]


def wrap_pad(masked):
    wrapped = jnp.concatenate([masked[-1:], masked, masked[:1]], axis=0)
    return jnp.pad(wrapped, ((0, 0), (1, 1), (1, 1)))


def remainder_of(field, source, fluid, diagonal):
    beside_all = face_sum(wrap_pad(fluid * field))
    return source - (diagonal * field - fluid * beside_all)


def jacobi_sweep(field, source, fluid, diagonal):
    return field + DAMPING * remainder_of(field, source, fluid, diagonal) / diagonal


def reference(forcing, absorption, blocks):
    fluids = [expand(blocks)]
    absorbs = [absorption]
    for level_no in range(1, LEVELS):
        fluids.append(coarsen(fluids[-1], jnp.max))
        absorbs.append(coarsen(absorbs[-1], jnp.sum) * 0.25)
    diagonals = [fl * (6.0 + ab) + 1.0 - fl for fl, ab in zip(fluids, absorbs)]

    def vcycle(level_no, field, source):
        fluid = fluids[level_no]
        diagonal = diagonals[level_no]
        if level_no == LEVELS - 1:
            for sweep_no in range(COARSE_SWEEPS):
                field = jacobi_sweep(field, source, fluid, diagonal)
            return field
        for sweep_no in range(SWEEPS):
            field = jacobi_sweep(field, source, fluid, diagonal)
        remainder = remainder_of(field, source, fluid, diagonal)
        coarse_src = coarsen(remainder, jnp.sum) * 0.25
        correction = vcycle(level_no + 1, jnp.zeros_like(coarse_src), coarse_src)
        field = field + fluid * refine(correction)
        for sweep_no in range(SWEEPS):
            field = jacobi_sweep(field, source, fluid, diagonal)
        return field

    pressure = jnp.zeros_like(forcing)
    for cycle_no in range(CYCLES):
        pressure = vcycle(0, pressure, forcing)
    residual = remainder_of(pressure, forcing, fluids[0], diagonals[0])
    return pressure, residual
```

```python
import functools
import jax
import jax.numpy as jnp
from jax import lax
from jax.experimental import pallas as pl
from jax.experimental.pallas import tpu as pltpu
from jax.sharding import PartitionSpec as P

MESH = pl.DeviceIdType.MESH
H = 4
BASE = 12
DAMP = 0.8
KEEP = 0.2
SENDS = 136


def kernel(ng, nz, A, X, f_in, a_in, m_in, p_out, r_out,
           SWF, SWA, SWM, FS, AB, FL, DG, CC, BB, WA, WB, V, V3, RT, TMP,
           SG0, RG0, A1, F1, D1, C1, B1, S1, W1A, W1B, G1S, G1R,
           GL, GA, GB, D2, F2, A2, C2, S2, B2, W2A, W2B, LOC2, T2, AB3, C3, B3, W3A, W3B,
           OST, send_sem, recv_sem):
    az, z, p = lax.axis_index("azim"), lax.axis_index("axial"), lax.axis_index("pair")
    g = az * 2 + p
    own = A // 2
    X1, X2L = X // 2, X // 4
    n2a, x2, n3a, x3 = ng * 2, nz * X2L, ng, nz * X2L // 2
    c3rows = (x3 + 7) // 8 * 8
    lane = lax.broadcasted_iota(jnp.int32, (1, 128), 1)
    counter = [0]

    def dev(gg, zz):
        return (gg // 2, zz, lax.rem(gg, 2))

    def gshift(o):
        return lax.rem(g + o + ng, ng)

    has_lo, has_hi = z > 0, z < nz - 1

    for ref in (FS, AB, FL, WA, WB, V3, A1, F1, W1A, W1B, W2A, W2B, W3A, W3B, C3, B3, AB3, LOC2):
        @pl.loop(0, ref.shape[1])
        def _(a, ref=ref):
            for h in range(2):
                ref[h, a] = jnp.zeros(ref.shape[2:], jnp.float32)
    for c in range(2):
        for h in range(2):
            S1[c, h] = jnp.zeros(S1.shape[2:], jnp.float32)
    bar = pltpu.get_barrier_semaphore()
    for o in range(1, ng):
        pl.semaphore_signal(bar, inc=1, device_id=dev(gshift(o), z), device_id_type=MESH)
    for o in range(1, nz):
        pl.semaphore_signal(bar, inc=1, device_id=dev(g, lax.rem(z + o, nz)), device_id_type=MESH)
    for cond, dz in ((has_lo, -1), (has_hi, 1)):
        @pl.when(cond)
        def _():
            for o in (-1, 1):
                pl.semaphore_signal(bar, inc=1, device_id=dev(gshift(o), z + dz), device_id_type=MESH)
    lows = jnp.where(has_lo, 2, 0) + jnp.where(has_hi, 2, 0)

    pl.semaphore_wait(bar, (ng - 1) + (nz - 1) + lows)

    def remote(src, dst, target, cond=None):
        k = counter[0]
        counter[0] += 1
        def make():
            return pltpu.make_async_remote_copy(
                src_ref=src, dst_ref=dst, send_sem=send_sem.at[k], recv_sem=recv_sem.at[k],
                device_id=target, device_id_type=MESH)
        if cond is None:
            make().start()
        else:
            pl.when(cond)(lambda: make().start())
        return make

    def finish(pairs):
        for make, cs, cr in pairs:
            if cs is None:
                make().wait_send()
                make().wait_recv()
            else:
                pl.when(cs)(lambda make=make: make().wait_send())
                pl.when(cr)(lambda make=make: make().wait_recv())

    def partner(y, s):
        return jnp.where((lane // s) % 2 == 0, pltpu.roll(y, 128 - s, 1), pltpu.roll(y, s, 1))

    def halo_start(buf, stg, rcv, ha, n, r0, nrows, hs=None):
        hs = ha if hs is None else hs
        last = BASE + nrows - H
        @pl.loop(0, n)
        def _(a):
            for h in range(2):
                stg[0, h, a] = buf[h, ha + a, BASE:BASE + H]
                stg[1, h, a] = buf[h, ha + a, last:last + H]
        end = r0
        out = []
        for o in (-1, 1):
            s0 = ha if o < 0 else ha + n - hs
            d0 = ha + n if o < 0 else ha - hs
            out.append((remote(buf.at[:, pl.ds(s0, hs), pl.ds(8, end)],
                               buf.at[:, pl.ds(d0, hs), pl.ds(8, end)],
                               dev(gshift(o), z)), None, None))
        for side, dz, cs, cr in ((0, -1, has_lo, has_hi), (1, 1, has_hi, has_lo)):
            for o in (-1, 0, 1):
                if o == 0:
                    src = stg.at[side]
                    dst = rcv.at[1 - side, :, pl.ds(ha, n)]
                else:
                    s0 = 0 if o < 0 else n - hs
                    d0 = ha + n if o < 0 else ha - hs
                    src = stg.at[side, :, pl.ds(s0, hs)]
                    dst = rcv.at[1 - side, :, pl.ds(d0, hs)]
                out.append((remote(src, dst, dev(gshift(o), z + dz), cs), cs, cr))
        return out

    def halo_place(buf, rcv, ha, n, nrows, hs=None):
        hs = ha if hs is None else hs
        for side, cond, row in ((0, has_lo, BASE - H), (1, has_hi, BASE + nrows)):
            @pl.when(cond)
            def _():
                @pl.loop(ha - hs, n + ha + hs)
                def _(a):
                    for h in range(2):
                        buf[h, a, row:row + H] = rcv[side, h, a]
            @pl.when(jnp.logical_not(cond))
            def _():
                @pl.loop(ha - hs, n + ha + hs)
                def _(a):
                    for h in range(2):
                        buf[h, a, row:row + H] = jnp.zeros((H, 128), jnp.float32)

    def beside(buf, a, up, dn, r0, n, s):
        cen = [buf[h, a, pl.ds(r0, n)] for h in range(2)]
        lf = [pltpu.roll(v, s, 1) for v in cen]
        rt = [pltpu.roll(v, 128 - s, 1) for v in cen]
        left = [jnp.where(lane < s, 0.0, lf[0]), jnp.where(lane < s, lf[0], lf[1])]
        right = [jnp.where(lane >= 128 - s, rt[1], rt[0]), jnp.where(lane >= 128 - s, 0.0, rt[1])]
        tot = []
        for h in range(2):
            t = buf[h, up, pl.ds(r0, n)] + buf[h, dn, pl.ds(r0, n)]
            t = t + buf[h, a, pl.ds(r0 + 1, n)] + buf[h, a, pl.ds(r0 - 1, n)]
            tot.append(t + left[h] + right[h])
        return cen, tot

    def sweep(dst, src, b, c, lo, hi, r0, n, s, ring=None, bidx=None):
        @pl.loop(lo, hi)
        def _(a):
            up, dn = (a + 1, a - 1) if ring is None else (lax.rem(a + 1, ring), lax.rem(a + ring - 1, ring))
            cen, tot = beside(src, a, up, dn, r0, n, s)
            for h in range(2):
                dst[h, a, pl.ds(r0, n)] = (KEEP * cen[h] + b[h, a, pl.ds(r0, n)]
                                           + c[h, a, pl.ds(r0, n)] * tot[h])

    other = 1 - p
    sib = (az, z, other)
    mo = own // 4
    sw = []
    for src, dst, n in ((f_in, SWF, own), (a_in, SWA, own), (m_in, SWM, mo)):
        sw.append((remote(src.at[pl.ds(other * n, n)], dst, sib), None, None))
    PXR = X + 2 * H
    P1R = 32

    for src, dst, n, ha in ((f_in, FS, own, H), (a_in, AB, own, H), (m_in, FL, mo, 1)):
        @pl.loop(0, n)
        def _(a, src=src, dst=dst, n=n, ha=ha):
            dst[p, ha + a, BASE:BASE + X] = src[p * n + a]
    finish(sw)
    for src, dst, n, ha in ((SWF, FS, own, H), (SWA, AB, own, H), (SWM, FL, mo, 1)):
        @pl.loop(0, n)
        def _(a, src=src, dst=dst, n=n, ha=ha):
            dst[other, ha + a, BASE:BASE + X] = src[a]

    flight = []
    stages = {}
    for i, (buf, ha, n) in enumerate(((FS, H, own), (AB, H, own), (FL, 1, mo))):
        flight += halo_start(buf, SG0.at[i, :, :, pl.ds(0, n)],
                             RG0.at[i, :, :, pl.ds(0, n + 2 * ha)], ha, n, PXR, X)

    def rows2(n, r0, op):
        return op(TMP[pl.ds(r0, n, stride=2)], TMP[pl.ds(r0 + 1, n, stride=2)])

    @pl.loop(0, own // 2)
    def _(k):
        for h in range(2):
            TMP[0:PXR] = AB[h, H + 2 * k, 8:8 + PXR] + AB[h, H + 2 * k + 1, 8:8 + PXR]
            t = rows2(X1, BASE - 8, jnp.add)
            A1[h, H + k, BASE:BASE + X1] = 0.25 * (t + partner(t, 1))
            TMP[0:PXR] = FL[h, 1 + k // 2, 8:8 + PXR]
            F1[h, H + k, BASE:BASE + X1] = TMP[pl.ds(BASE - 8, X1, stride=2)]
    for i, buf in enumerate((A1, F1)):
        flight += halo_start(buf, G1S.at[i], G1R.at[i], H, own // 2, P1R, X1)

    def restrict2(buf, h, k, op):
        TMP[0:P1R] = op(buf[h, 2 * k, 8:8 + P1R], buf[h, 2 * k + 1, 8:8 + P1R])
        t = rows2(X2L, BASE - 8, op)
        return op(t, partner(t, 2))

    def put(slot, vals):
        y = jnp.where(lane % 4 == 0, vals[0], jnp.where(lane % 4 == 1, vals[1], jnp.where(lane % 4 == 2, vals[2], vals[3])))
        GL[slot, 0:X2L] = y

    def gather(slot, count):
        rs = []
        @pl.loop(0, count)
        def _(i):
            GA[slot + i, z] = GL[slot + i]
        for o in range(1, nz):
            rs.append((remote(GL.at[pl.ds(slot, count)], GA.at[pl.ds(slot, count), z],
                              dev(g, lax.rem(z + o, nz))), None, None))
        finish(rs)
        rs = []
        for o in range(1, ng):
            rs.append((remote(GA.at[pl.ds(slot, count)], GB.at[pl.ds(slot, count), g],
                              dev(gshift(o), z)), None, None))
        for i in range(count):
            for zz in range(nz):
                GB[slot + i, g, zz] = GA[slot + i, zz]
        finish(rs)

    def unpack(slot, dst):
        @pl.loop(0, ng)
        def _(gg):
            for zz in range(nz):
                t = GB[slot, gg, zz]
                for q in range(4):
                    y = jnp.where(lane % 4 == q, t, 0.0)
                    y = y + partner(y, 1)
                    y = y + partner(y, 2)
                    dst[q // 2, 2 * gg + q % 2, pl.ds(8 + X2L * zz, X2L)] = y[0:X2L]

    vals = [0.25 * restrict2(A1.at[:, pl.ds(H, own // 2)], q // 2, q % 2, jnp.add) for q in range(4)]
    put(0, vals)
    vals = [restrict2(F1.at[:, pl.ds(H, own // 2)], q // 2, q % 2, jnp.maximum) for q in range(4)]
    put(1, vals)
    gather(0, 2)
    unpack(0, A2)
    unpack(1, F2)

    R2 = x2
    @pl.loop(0, n2a)
    def _(a):
        for h in range(2):
            f = F2[h, a, pl.ds(8, R2)]
            d = f * (6.0 + A2[h, a, pl.ds(8, R2)]) + 1.0 - f
            D2[h, a, pl.ds(8, R2)] = d
            C2[h, a, pl.ds(8, R2)] = DAMP * f / d

    @pl.loop(0, n3a)
    def _(k):
        for h in range(2):
            T2[0:R2] = A2[h, 2 * k, pl.ds(8, R2)] + A2[h, 2 * k + 1, pl.ds(8, R2)]
            t = T2[pl.ds(0, x3, stride=2)] + T2[pl.ds(1, x3, stride=2)]
            ab = 0.25 * (t + partner(t, 4))
            T2[0:R2] = jnp.maximum(F2[h, 2 * k, pl.ds(8, R2)], F2[h, 2 * k + 1, pl.ds(8, R2)])
            t = jnp.maximum(T2[pl.ds(0, x3, stride=2)], T2[pl.ds(1, x3, stride=2)])
            f = jnp.maximum(t, partner(t, 4))
            C3[h, k, 8:8 + x3] = DAMP * f / (f * (6.0 + ab) + 1.0 - f)

    finish(flight)
    for i, (buf, ha, n) in enumerate(((FS, H, own), (AB, H, own), (FL, 1, mo))):
        halo_place(buf, RG0.at[i, :, :, pl.ds(0, n + 2 * ha)], ha, n, X)
    for i, buf in enumerate((A1, F1)):
        halo_place(buf, G1R.at[i], H, own // 2, X1)

    @pl.loop(0, own + 2 * H)
    def _(a):
        for h in range(2):
            f = FL[h, a // 4, 8:8 + PXR]
            d = f * (6.0 + AB[h, a, 8:8 + PXR]) + 1.0 - f
            c = DAMP * f / d
            DG[h, a, 8:8 + PXR] = d
            CC[h, a, 8:8 + PXR] = c
            BB[h, a, 8:8 + PXR] = c * FS[h, a, 8:8 + PXR]

    @pl.loop(0, own // 2 + 2 * H)
    def _(a):
        for h in range(2):
            f = F1[h, a, 8:8 + P1R]
            d = f * (6.0 + A1[h, a, 8:8 + P1R]) + 1.0 - f
            D1[h, a, 8:8 + P1R] = d
            C1[h, a, 8:8 + P1R] = DAMP * f / d

    def remainder0(buf, a, solid):
        cen, tot = beside(buf, a, a + 1, a - 1, 8, PXR, 1)
        out = []
        for h in range(2):
            f = FL[h, a // 4, 8:8 + PXR]
            s = FS[h, a, 8:8 + PXR]
            out.append(jnp.where(f > 0, s - (DG[h, a, 8:8 + PXR] * cen[h] - tot[h]), solid * s))
        return out

    def level3():
        @pl.loop(0, n3a)
        def _(a):
            for h in range(2):
                W3A[h, a, pl.ds(8, c3rows)] = B3[h, a, pl.ds(8, c3rows)]
        for src, dst in ((W3A, W3B), (W3B, W3A), (W3A, W3B)):
            sweep(dst, src, B3, C3, 0, n3a, 8, c3rows, 8, ring=n3a)
        return W3B

    def level2():
        @pl.loop(0, n2a)
        def _(a):
            for h in range(2):
                b = C2[h, a, pl.ds(8, R2)] * S2[h, a, pl.ds(8, R2)]
                B2[h, a, pl.ds(8, R2)] = b
                W2A[h, a, pl.ds(8, R2)] = b
        sweep(W2B, W2A, B2, C2, 0, n2a, 8, R2, 4, ring=n2a)

        @pl.loop(0, n3a)
        def _(k):
            rem = [0.0, 0.0]
            for j in range(2):
                a = 2 * k + j
                cen, tot = beside(W2B, a, lax.rem(a + 1, n2a), lax.rem(a + n2a - 1, n2a), 8, R2, 4)
                for h in range(2):
                    s = S2[h, a, pl.ds(8, R2)]
                    rem[h] = rem[h] + jnp.where(F2[h, a, pl.ds(8, R2)] > 0,
                                                s - (D2[h, a, pl.ds(8, R2)] * cen[h] - tot[h]), (KEEP * KEEP) * s)
            for h in range(2):
                T2[0:R2] = rem[h]
                t = T2[pl.ds(0, x3, stride=2)] + T2[pl.ds(1, x3, stride=2)]
                B3[h, k, 8:8 + x3] = C3[h, k, 8:8 + x3] * (0.25 * (t + partner(t, 4)))
        w3 = level3()

        @pl.loop(0, n3a)
        def _(k):
            for h in range(2):
                v = w3[h, k, 8:8 + x3]
                T2[pl.ds(0, x3, stride=2)] = v
                T2[pl.ds(1, x3, stride=2)] = v
                t = T2[0:R2]
                for j in range(2):
                    W2A[h, 2 * k + j, pl.ds(8, R2)] = W2B[h, 2 * k + j, pl.ds(8, R2)] + F2[h, 2 * k + j, pl.ds(8, R2)] * t
        sweep(W2B, W2A, B2, C2, 0, n2a, 8, R2, 4, ring=n2a)
        sweep(W2A, W2B, B2, C2, 0, n2a, 8, R2, 4, ring=n2a)
        return W2A

    def level1(cyc):
        src = S1.at[cyc]
        fl = halo_start(src, G1S.at[2 + cyc], G1R.at[2 + cyc], H, own // 2, P1R, X1)
        finish(fl)
        halo_place(src, G1R.at[2 + cyc], H, own // 2, X1)
        n1 = own // 2 + 2 * H

        @pl.loop(0, n1)
        def _(a):
            for h in range(2):
                b = C1[h, a, 8:8 + P1R] * src[h, a, 8:8 + P1R]
                B1[h, a, 8:8 + P1R] = b
                W1A[h, a, 8:8 + P1R] = b
        sweep(W1B, W1A, B1, C1, 1, n1 - 1, 8, P1R, 2)

        vals = {}
        for k in range(2):
            rem = [0.0, 0.0]
            for j in range(2):
                a = H + 2 * k + j
                cen, tot = beside(W1B, a, a + 1, a - 1, 8, P1R, 2)
                for h in range(2):
                    s = src[h, a, 8:8 + P1R]
                    rem[h] = rem[h] + jnp.where(F1[h, a, 8:8 + P1R] > 0,
                                                s - (D1[h, a, 8:8 + P1R] * cen[h] - tot[h]), (KEEP * KEEP) * s)
            for h in range(2):
                TMP[0:P1R] = rem[h]
                t = rows2(X2L, BASE - 8, jnp.add)
                vals[(h, k)] = 0.25 * (t + partner(t, 2))
        put(2 + cyc, [vals[(q // 2, q % 2)] for q in range(4)])
        gather(2 + cyc, 1)
        unpack(2 + cyc, S2)
        w2 = level2()
        nl = own // 4 + 4
        for zz in range(nz):
            @pl.when(z == zz)
            def _(zz=zz):
                @pl.loop(0, nl)
                def _(j):
                    a = lax.rem(own // 4 * g + j - 2 + n2a, n2a)
                    for h in range(2):
                        LOC2[h, j, 0:16] = w2[h, a, 8 + X2L * zz - 2:8 + X2L * zz + 14]

        @pl.loop(0, nl)
        def _(j):
            for h in range(2):
                v = LOC2[h, j, 0:16]
                TMP[pl.ds(0, 16, stride=2)] = v
                TMP[pl.ds(1, 16, stride=2)] = v
                t = TMP[0:P1R]
                for i in range(2):
                    a = 2 * j + i
                    W1A[h, a, 8:8 + P1R] = W1B[h, a, 8:8 + P1R] + F1[h, a, 8:8 + P1R] * t
        sweep(W1B, W1A, B1, C1, 2, n1 - 2, 8, P1R, 2)
        sweep(W1A, W1B, B1, C1, 3, n1 - 3, 8, P1R, 2)
        return W1A

    n0 = own + 2 * H
    for cyc in range(2):
        if cyc == 0:
            sweep(WB, BB, BB, CC, 2, n0 - 2, 8, PXR, 1)
        else:
            fl = halo_start(V, SG0.at[3], RG0.at[3], H, own, PXR, X)
            finish(fl)
            halo_place(V, RG0.at[3], H, own, X)
            sweep(WA, V, BB, CC, 1, n0 - 1, 8, PXR, 1)
            sweep(WB, WA, BB, CC, 2, n0 - 2, 8, PXR, 1)
        solid = KEEP ** (2 if cyc == 0 else 6)

        @pl.loop(0, own // 2)
        def _(k):
            ra = remainder0(WB, H + 2 * k, solid)
            rb = remainder0(WB, H + 2 * k + 1, solid)
            for h in range(2):
                TMP[0:PXR] = ra[h] + rb[h]
                t = rows2(X1, BASE - 8, jnp.add)
                S1[cyc, h, H + k, BASE:BASE + X1] = 0.25 * (t + partner(t, 1))
        w1 = level1(cyc)

        @pl.loop(3, own // 2 + 2 * H - 3)
        def _(k):
            for h in range(2):
                v = w1[h, k, BASE - 2:BASE - 2 + X1 + 4]
                TMP[pl.ds(0, X1 + 4, stride=2)] = v
                TMP[pl.ds(1, X1 + 4, stride=2)] = v
                t = TMP[0:PXR]
                for i in range(2):
                    a = 2 * (k - 2) + i
                    WA[h, a, 8:8 + PXR] = WB[h, a, 8:8 + PXR] + jnp.where(FL[h, a // 4, 8:8 + PXR] > 0, t, 0.0)
        sweep(WB, WA, BB, CC, 3, n0 - 3, 8, PXR, 1)
        sweep(V if cyc == 0 else V3, WB, BB, CC, 4, n0 - 4, 8, PXR, 1)

    fl = halo_start(V3, SG0.at[4], RG0.at[4], H, own, PXR, X, hs=1)
    grown = 1.0 - KEEP ** 8

    @pl.loop(0, own)
    def _(a):
        for h in range(2):
            f = FL[h, 1 + a // 4, BASE:BASE + X]
            OST[0, h, a] = jnp.where(f > 0, V3[h, H + a, BASE:BASE + X], grown * FS[h, H + a, BASE:BASE + X])
    outs = [(remote(OST.at[0, other], p_out.at[pl.ds(p * own, own)], sib), None, None)]
    finish(fl)
    halo_place(V3, RG0.at[4], H, own, X, hs=1)

    @pl.loop(0, own)
    def _(a):
        r = remainder0(V3, H + a, KEEP ** 8)
        for h in range(2):
            OST[1, h, a] = r[h][H:H + X]
    outs.append((remote(OST.at[1, other], r_out.at[pl.ds(p * own, own)], sib), None, None))

    @pl.loop(0, own)
    def _(a):
        p_out[p * own + a] = OST[0, p, a]
        r_out[p * own + a] = OST[1, p, a]
    finish(outs)


def solution(mesh):
    ng = mesh.shape["azim"] * mesh.shape["pair"]
    nz = mesh.shape["axial"]

    def per_device(forcing, absorption, blocks):
        A, X, R = forcing.shape
        own = A // 2
        fl = jnp.repeat(jnp.repeat(blocks.astype(jnp.float32), 4, axis=1), 4, axis=2)
        px, p1 = X + 24, 48
        n0, n1 = own + 2 * H, own // 2 + 2 * H
        x2 = nz * (X // 4)
        n2, r2 = ng * 2, x2 + 16
        n3, r3 = ng, (x2 // 2 + 7) // 8 * 8 + 16
        V = lambda *s: pltpu.VMEM(s, jnp.float32)
        full = V(2, n0, px, 128)
        lev1 = V(2, n1, p1, 128)
        lev2 = V(2, n2, r2, 128)
        lev3 = V(2, n3, r3, 128)
        scratch = [
            V(own, X, 128), V(own, X, 128), V(own // 4, X, 128),
            full, full, V(2, own // 4 + 2, px, 128),
            full, full, full, full, full, full, full, V(8, 128), V(64, 128),
            V(5, 2, 2, own, H, 128), V(5, 2, 2, n0, H, 128),
            lev1, lev1, lev1, lev1, lev1, V(2, 2, n1, p1, 128), lev1, lev1,
            V(4, 2, 2, own // 2, H, 128), V(4, 2, 2, n1, H, 128),
            V(4, 16, 128), V(4, nz, 16, 128), V(4, ng, nz, 16, 128),
            lev2, lev2, lev2, lev2, lev2, lev2, lev2, lev2,
            V(2, own // 4 + 4, 16, 128), V(x2, 128), V(2, 1, 8, 128), lev3, lev3, lev3, lev3,
            V(2, 2, own, X, 128),
            pltpu.SemaphoreType.DMA((SENDS,)), pltpu.SemaphoreType.DMA((SENDS,)),
        ]
        vm = pl.BlockSpec(memory_space=pltpu.VMEM)
        return pl.pallas_call(
            functools.partial(kernel, ng, nz, A, X),
            out_shape=[jax.ShapeDtypeStruct((A, X, R), jnp.float32)] * 2,
            in_specs=[vm] * 3, out_specs=[vm] * 2, scratch_shapes=scratch,
            compiler_params=pltpu.CompilerParams(
                collective_id=0, has_side_effects=True, vmem_limit_bytes=56 * 1024 * 1024),
        )(forcing, absorption, fl)

    spec = P("azim", "axial", "pair")
    return jax.shard_map(per_device, mesh=mesh, in_specs=(spec,) * 3, out_specs=(spec,) * 2, check_vma=False)
```

```python
import functools
import jax
import jax.numpy as jnp
from jax import lax
from jax.experimental import pallas as pl
from jax.experimental.pallas import tpu as pltpu
from jax.sharding import PartitionSpec as P

MESH = pl.DeviceIdType.MESH
H = 4
BASE = 12
DAMP = 0.8
KEEP = 0.2
SENDS = 136


def kernel(ng, nz, A, X, f_in, a_in, m_in, p_out, r_out,
           SWF, SWA, SWM, FS, AB, FL, DG, CC, BB, WA, WB, V, V3, RT, TMP,
           SG0, RG0, A1, F1, D1, C1, B1, S1, W1A, W1B, G1S, G1R,
           GL, GA, GB, D2, F2, A2, C2, S2, B2, W2A, W2B, LOC2, T2, AF, C3, B3, W3A, W3B,
           OST, send_sem, recv_sem):
    az, z, p = lax.axis_index("azim"), lax.axis_index("axial"), lax.axis_index("pair")
    g = az * 2 + p
    own = A // 2
    X1, X2L = X // 2, X // 4
    n2a, x2, n3a, x3 = ng * 2, nz * X2L, ng, nz * X2L // 2
    c3rows = (x3 + 7) // 8 * 8
    lane = lax.broadcasted_iota(jnp.int32, (1, 128), 1)
    counter = [0]

    def dev(gg, zz):
        return (gg // 2, zz, lax.rem(gg, 2))

    def gshift(o):
        return lax.rem(g + o + ng, ng)

    has_lo, has_hi = z > 0, z < nz - 1

    for ref in (WA, WB, AF, W1A, W1B, W2A, W2B, W3A, W3B, C3, B3):
        @pl.loop(0, ref.shape[1])
        def _(a, ref=ref):
            for h in range(2):
                ref[h, a] = jnp.zeros(ref.shape[2:], jnp.float32)
    for c in range(2):
        for h in range(2):
            S1[c, h] = jnp.zeros(S1.shape[2:], jnp.float32)
    bar = pltpu.get_barrier_semaphore()
    for o in range(1, ng):
        pl.semaphore_signal(bar, inc=1, device_id=dev(gshift(o), z), device_id_type=MESH)
    for o in range(1, nz):
        pl.semaphore_signal(bar, inc=1, device_id=dev(g, lax.rem(z + o, nz)), device_id_type=MESH)
    for cond, dz in ((has_lo, -1), (has_hi, 1)):
        @pl.when(cond)
        def _():
            for o in (-1, 1):
                pl.semaphore_signal(bar, inc=1, device_id=dev(gshift(o), z + dz), device_id_type=MESH)
    lows = jnp.where(has_lo, 2, 0) + jnp.where(has_hi, 2, 0)

    pl.semaphore_wait(bar, (ng - 1) + (nz - 1) + lows)

    def remote(src, dst, target, cond=None):
        k = counter[0]
        counter[0] += 1
        def make():
            return pltpu.make_async_remote_copy(
                src_ref=src, dst_ref=dst, send_sem=send_sem.at[k], recv_sem=recv_sem.at[k],
                device_id=target, device_id_type=MESH)
        if cond is None:
            make().start()
        else:
            pl.when(cond)(lambda: make().start())
        return make

    def finish(pairs):
        for make, cs, cr in pairs:
            if cs is None:
                make().wait_send()
                make().wait_recv()
            else:
                pl.when(cs)(lambda make=make: make().wait_send())
                pl.when(cr)(lambda make=make: make().wait_recv())

    def partner(y, s):
        return jnp.where((lane // s) % 2 == 0, pltpu.roll(y, 128 - s, 1), pltpu.roll(y, s, 1))

    def halo_start(buf, stg, rcv, ha, n, r0, nrows, hs=None):
        hs = ha if hs is None else hs
        last = BASE + nrows - H
        @pl.loop(0, n)
        def _(a):
            for h in range(2):
                stg[0, h, a] = buf[h, ha + a, BASE:BASE + H]
                stg[1, h, a] = buf[h, ha + a, last:last + H]
        end = r0
        out = []
        for o in (-1, 1):
            s0 = ha if o < 0 else ha + n - hs
            d0 = ha + n if o < 0 else ha - hs
            out.append((remote(buf.at[:, pl.ds(s0, hs), pl.ds(8, end)],
                               buf.at[:, pl.ds(d0, hs), pl.ds(8, end)],
                               dev(gshift(o), z)), None, None))
        for side, dz, cs, cr in ((0, -1, has_lo, has_hi), (1, 1, has_hi, has_lo)):
            for o in (-1, 0, 1):
                if o == 0:
                    src = stg.at[side]
                    dst = rcv.at[1 - side, :, pl.ds(ha, n)]
                else:
                    s0 = 0 if o < 0 else n - hs
                    d0 = ha + n if o < 0 else ha - hs
                    src = stg.at[side, :, pl.ds(s0, hs)]
                    dst = rcv.at[1 - side, :, pl.ds(d0, hs)]
                out.append((remote(src, dst, dev(gshift(o), z + dz), cs), cs, cr))
        return out

    def halo_place(buf, rcv, ha, n, nrows, hs=None):
        hs = ha if hs is None else hs
        for side, cond, row in ((0, has_lo, BASE - H), (1, has_hi, BASE + nrows)):
            @pl.when(cond)
            def _():
                @pl.loop(ha - hs, n + ha + hs)
                def _(a):
                    for h in range(2):
                        buf[h, a, row:row + H] = rcv[side, h, a]
            @pl.when(jnp.logical_not(cond))
            def _():
                @pl.loop(ha - hs, n + ha + hs)
                def _(a):
                    for h in range(2):
                        buf[h, a, row:row + H] = jnp.zeros((H, 128), jnp.float32)

    def beside(buf, a, up, dn, r0, n, s):
        cen = [buf[h, a, pl.ds(r0, n)] for h in range(2)]
        lf = [pltpu.roll(v, s, 1) for v in cen]
        rt = [pltpu.roll(v, 128 - s, 1) for v in cen]
        left = [jnp.where(lane < s, 0.0, lf[0]), jnp.where(lane < s, lf[0], lf[1])]
        right = [jnp.where(lane >= 128 - s, rt[1], rt[0]), jnp.where(lane >= 128 - s, 0.0, rt[1])]
        tot = []
        for h in range(2):
            t = buf[h, up, pl.ds(r0, n)] + buf[h, dn, pl.ds(r0, n)]
            t = t + buf[h, a, pl.ds(r0 + 1, n)] + buf[h, a, pl.ds(r0 - 1, n)]
            tot.append(t + left[h] + right[h])
        return cen, tot

    def sweep(dst, src, b, c, lo, hi, r0, n, s, ring=None, bidx=None):
        @pl.loop(lo, hi, unroll=4)
        def _(a):
            up, dn = (a + 1, a - 1) if ring is None else (lax.rem(a + 1, ring), lax.rem(a + ring - 1, ring))
            cen, tot = beside(src, a, up, dn, r0, n, s)
            for h in range(2):
                dst[h, a, pl.ds(r0, n)] = (KEEP * cen[h] + b[h, a, pl.ds(r0, n)]
                                           + c[h, a, pl.ds(r0, n)] * tot[h])

    other = 1 - p
    sib = (az, z, other)
    mo = own // 4
    sw = []
    for src, dst, n in ((f_in, SWF, own), (a_in, SWA, own), (m_in, SWM, mo)):
        sw.append((remote(src.at[pl.ds(other * n, n)], dst, sib), None, None))
    PXR = X + 2 * H
    P1R = 32

    for src, dst, n, ha in ((f_in, FS, own, H), (a_in, AB, own, H), (m_in, FL, mo, 1)):
        @pl.loop(0, n)
        def _(a, src=src, dst=dst, n=n, ha=ha):
            dst[p, ha + a, BASE:BASE + X] = src[p * n + a]
    finish(sw)
    for src, dst, n, ha in ((SWF, FS, own, H), (SWA, AB, own, H), (SWM, FL, mo, 1)):
        @pl.loop(0, n)
        def _(a, src=src, dst=dst, n=n, ha=ha):
            dst[other, ha + a, BASE:BASE + X] = src[a]

    flight = []
    stages = {}
    for i, (buf, ha, n) in enumerate(((FS, H, own), (AB, H, own), (FL, 1, mo))):
        flight += halo_start(buf, SG0.at[i, :, :, pl.ds(0, n)],
                             RG0.at[i, :, :, pl.ds(0, n + 2 * ha)], ha, n, PXR, X, hs=min(ha, H - 1))

    def rows2(n, r0, op):
        return op(TMP[pl.ds(r0, n, stride=2)], TMP[pl.ds(r0 + 1, n, stride=2)])

    @pl.loop(0, own // 2)
    def _(k):
        for h in range(2):
            TMP[0:PXR] = AB[h, H + 2 * k, 8:8 + PXR] + AB[h, H + 2 * k + 1, 8:8 + PXR]
            t = rows2(X1, BASE - 8, jnp.add)
            ab = 0.25 * (t + partner(t, 1))
            A1[h, H + k, BASE:BASE + X1] = ab
            TMP[0:PXR] = FL[h, 1 + k // 2, 8:8 + PXR]
            f = TMP[pl.ds(BASE - 8, X1, stride=2)]
            F1[h, H + k, BASE:BASE + X1] = f
            AF[h, H + k, BASE:BASE + X1] = jnp.where(lane % 2 == 0, ab, f)
    flight += halo_start(AF, G1S.at[0], G1R.at[0], H, own // 2, P1R, X1)

    def restrict2(buf, h, k, op):
        TMP[0:P1R] = op(buf[h, 2 * k, 8:8 + P1R], buf[h, 2 * k + 1, 8:8 + P1R])
        t = rows2(X2L, BASE - 8, op)
        return op(t, partner(t, 2))

    def put(slot, vals):
        y = jnp.where(lane % 4 == 0, vals[0], jnp.where(lane % 4 == 1, vals[1], jnp.where(lane % 4 == 2, vals[2], vals[3])))
        GL[slot, 0:X2L] = y

    def gather(slot, count):
        rs = []
        @pl.loop(0, count)
        def _(i):
            GA[slot + i, z] = GL[slot + i]
        for o in range(1, nz):
            rs.append((remote(GL.at[pl.ds(slot, count)], GA.at[pl.ds(slot, count), z],
                              dev(g, lax.rem(z + o, nz))), None, None))
        finish(rs)
        rs = []
        for o in range(1, ng):
            rs.append((remote(GA.at[pl.ds(slot, count)], GB.at[pl.ds(slot, count), g],
                              dev(gshift(o), z)), None, None))
        for i in range(count):
            for zz in range(nz):
                GB[slot + i, g, zz] = GA[slot + i, zz]
        finish(rs)

    def unpack(slot, dst):
        @pl.loop(0, ng)
        def _(gg):
            for zz in range(nz):
                t = GB[slot, gg, zz]
                for q in range(4):
                    y = jnp.where(lane % 4 == q, t, 0.0)
                    y = y + partner(y, 1)
                    y = y + partner(y, 2)
                    dst[q // 2, 2 * gg + q % 2, pl.ds(8 + X2L * zz, X2L)] = y[0:X2L]

    vals = [0.25 * restrict2(A1.at[:, pl.ds(H, own // 2)], q // 2, q % 2, jnp.add) for q in range(4)]
    put(0, vals)
    vals = [restrict2(F1.at[:, pl.ds(H, own // 2)], q // 2, q % 2, jnp.maximum) for q in range(4)]
    put(1, vals)
    gather(0, 2)
    unpack(0, A2)
    unpack(1, F2)

    R2 = x2
    @pl.loop(0, n2a)
    def _(a):
        for h in range(2):
            f = F2[h, a, pl.ds(8, R2)]
            d = f * (6.0 + A2[h, a, pl.ds(8, R2)]) + 1.0 - f
            D2[h, a, pl.ds(8, R2)] = d
            C2[h, a, pl.ds(8, R2)] = DAMP * f / d

    @pl.loop(0, n3a)
    def _(k):
        for h in range(2):
            T2[0:R2] = A2[h, 2 * k, pl.ds(8, R2)] + A2[h, 2 * k + 1, pl.ds(8, R2)]
            t = T2[pl.ds(0, x3, stride=2)] + T2[pl.ds(1, x3, stride=2)]
            ab = 0.25 * (t + partner(t, 4))
            T2[0:R2] = jnp.maximum(F2[h, 2 * k, pl.ds(8, R2)], F2[h, 2 * k + 1, pl.ds(8, R2)])
            t = jnp.maximum(T2[pl.ds(0, x3, stride=2)], T2[pl.ds(1, x3, stride=2)])
            f = jnp.maximum(t, partner(t, 4))
            C3[h, k, 8:8 + x3] = DAMP * f / (f * (6.0 + ab) + 1.0 - f)

    finish(flight)
    for i, (buf, ha, n) in enumerate(((FS, H, own), (AB, H, own), (FL, 1, mo))):
        halo_place(buf, RG0.at[i, :, :, pl.ds(0, n + 2 * ha)], ha, n, X, hs=min(ha, H - 1))
    halo_place(AF, G1R.at[0], H, own // 2, X1)

    @pl.loop(0, own + 2 * H)
    def _(a):
        for h in range(2):
            f = FL[h, a // 4, 8:8 + PXR]
            d = f * (6.0 + AB[h, a, 8:8 + PXR]) + 1.0 - f
            c = DAMP * f / d
            DG[h, a, 8:8 + PXR] = d
            CC[h, a, 8:8 + PXR] = c
            BB[h, a, 8:8 + PXR] = c * FS[h, a, 8:8 + PXR]

    @pl.loop(0, own // 2 + 2 * H)
    def _(a):
        for h in range(2):
            t = AF[h, a, 8:8 + P1R]
            swapped = partner(t, 1)
            f = jnp.where(lane % 2 == 0, swapped, t)
            F1[h, a, 8:8 + P1R] = f
            d = f * (6.0 + jnp.where(lane % 2 == 0, t, swapped)) + 1.0 - f
            D1[h, a, 8:8 + P1R] = d
            C1[h, a, 8:8 + P1R] = DAMP * f / d

    def remainder0(buf, a, solid):
        cen, tot = beside(buf, a, a + 1, a - 1, 8, PXR, 1)
        out = []
        for h in range(2):
            f = FL[h, a // 4, 8:8 + PXR]
            s = FS[h, a, 8:8 + PXR]
            out.append(jnp.where(f > 0, s - (DG[h, a, 8:8 + PXR] * cen[h] - tot[h]), solid * s))
        return out

    def level3():
        @pl.loop(0, n3a)
        def _(a):
            for h in range(2):
                W3A[h, a, pl.ds(8, c3rows)] = B3[h, a, pl.ds(8, c3rows)]
        for src, dst in ((W3A, W3B), (W3B, W3A), (W3A, W3B)):
            sweep(dst, src, B3, C3, 0, n3a, 8, c3rows, 8, ring=n3a)
        return W3B

    def level2():
        @pl.loop(0, n2a)
        def _(a):
            for h in range(2):
                b = C2[h, a, pl.ds(8, R2)] * S2[h, a, pl.ds(8, R2)]
                B2[h, a, pl.ds(8, R2)] = b
                W2A[h, a, pl.ds(8, R2)] = b
        sweep(W2B, W2A, B2, C2, 0, n2a, 8, R2, 4, ring=n2a)

        @pl.loop(0, n3a)
        def _(k):
            rem = [0.0, 0.0]
            for j in range(2):
                a = 2 * k + j
                cen, tot = beside(W2B, a, lax.rem(a + 1, n2a), lax.rem(a + n2a - 1, n2a), 8, R2, 4)
                for h in range(2):
                    s = S2[h, a, pl.ds(8, R2)]
                    rem[h] = rem[h] + jnp.where(F2[h, a, pl.ds(8, R2)] > 0,
                                                s - (D2[h, a, pl.ds(8, R2)] * cen[h] - tot[h]), (KEEP * KEEP) * s)
            for h in range(2):
                T2[0:R2] = rem[h]
                t = T2[pl.ds(0, x3, stride=2)] + T2[pl.ds(1, x3, stride=2)]
                B3[h, k, 8:8 + x3] = C3[h, k, 8:8 + x3] * (0.25 * (t + partner(t, 4)))
        w3 = level3()

        @pl.loop(0, n3a)
        def _(k):
            for h in range(2):
                v = w3[h, k, 8:8 + x3]
                T2[pl.ds(0, x3, stride=2)] = v
                T2[pl.ds(1, x3, stride=2)] = v
                t = T2[0:R2]
                for j in range(2):
                    W2A[h, 2 * k + j, pl.ds(8, R2)] = W2B[h, 2 * k + j, pl.ds(8, R2)] + F2[h, 2 * k + j, pl.ds(8, R2)] * t
        sweep(W2B, W2A, B2, C2, 0, n2a, 8, R2, 4, ring=n2a)
        sweep(W2A, W2B, B2, C2, 0, n2a, 8, R2, 4, ring=n2a)
        return W2A

    def level1(cyc):
        src = S1.at[cyc]
        fl = halo_start(src, G1S.at[2 + cyc], G1R.at[2 + cyc], H, own // 2, P1R, X1)
        finish(fl)
        halo_place(src, G1R.at[2 + cyc], H, own // 2, X1)
        n1 = own // 2 + 2 * H

        @pl.loop(0, n1)
        def _(a):
            for h in range(2):
                b = C1[h, a, 8:8 + P1R] * src[h, a, 8:8 + P1R]
                B1[h, a, 8:8 + P1R] = b
                W1A[h, a, 8:8 + P1R] = b
        sweep(W1B, W1A, B1, C1, 1, n1 - 1, 8, P1R, 2)

        vals = {}
        for k in range(2):
            rem = [0.0, 0.0]
            for j in range(2):
                a = H + 2 * k + j
                cen, tot = beside(W1B, a, a + 1, a - 1, 8, P1R, 2)
                for h in range(2):
                    s = src[h, a, 8:8 + P1R]
                    rem[h] = rem[h] + jnp.where(F1[h, a, 8:8 + P1R] > 0,
                                                s - (D1[h, a, 8:8 + P1R] * cen[h] - tot[h]), (KEEP * KEEP) * s)
            for h in range(2):
                TMP[0:P1R] = rem[h]
                t = rows2(X2L, BASE - 8, jnp.add)
                vals[(h, k)] = 0.25 * (t + partner(t, 2))
        put(2 + cyc, [vals[(q // 2, q % 2)] for q in range(4)])
        gather(2 + cyc, 1)
        unpack(2 + cyc, S2)
        w2 = level2()
        nl = own // 4 + 4
        for zz in range(nz):
            @pl.when(z == zz)
            def _(zz=zz):
                @pl.loop(0, nl)
                def _(j):
                    a = lax.rem(own // 4 * g + j - 2 + n2a, n2a)
                    for h in range(2):
                        LOC2[h, j, 0:16] = w2[h, a, 8 + X2L * zz - 2:8 + X2L * zz + 14]

        @pl.loop(0, nl)
        def _(j):
            for h in range(2):
                v = LOC2[h, j, 0:16]
                TMP[pl.ds(0, 16, stride=2)] = v
                TMP[pl.ds(1, 16, stride=2)] = v
                t = TMP[0:P1R]
                for i in range(2):
                    a = 2 * j + i
                    W1A[h, a, 8:8 + P1R] = W1B[h, a, 8:8 + P1R] + F1[h, a, 8:8 + P1R] * t
        sweep(W1B, W1A, B1, C1, 2, n1 - 2, 8, P1R, 2)
        sweep(W1A, W1B, B1, C1, 3, n1 - 3, 8, P1R, 2)
        return W1A

    n0 = own + 2 * H
    for cyc in range(2):
        if cyc == 0:
            sweep(WB, BB, BB, CC, 2, n0 - 2, 8, PXR, 1)
        else:
            fl = halo_start(V, SG0.at[3], RG0.at[3], H, own, PXR, X)
            finish(fl)
            halo_place(V, RG0.at[3], H, own, X)
            sweep(WA, V, BB, CC, 1, n0 - 1, 8, PXR, 1)
            sweep(WB, WA, BB, CC, 2, n0 - 2, 8, PXR, 1)
        solid = KEEP ** (2 if cyc == 0 else 6)

        @pl.loop(0, own // 2)
        def _(k):
            ra = remainder0(WB, H + 2 * k, solid)
            rb = remainder0(WB, H + 2 * k + 1, solid)
            for h in range(2):
                TMP[0:PXR] = ra[h] + rb[h]
                t = rows2(X1, BASE - 8, jnp.add)
                S1[cyc, h, H + k, BASE:BASE + X1] = 0.25 * (t + partner(t, 1))
        w1 = level1(cyc)

        @pl.loop(3, own // 2 + 2 * H - 3)
        def _(k):
            for h in range(2):
                v = w1[h, k, BASE - 2:BASE - 2 + X1 + 4]
                TMP[pl.ds(0, X1 + 4, stride=2)] = v
                TMP[pl.ds(1, X1 + 4, stride=2)] = v
                t = TMP[0:PXR]
                for i in range(2):
                    a = 2 * (k - 2) + i
                    WA[h, a, 8:8 + PXR] = WB[h, a, 8:8 + PXR] + jnp.where(FL[h, a // 4, 8:8 + PXR] > 0, t, 0.0)
        sweep(WB, WA, BB, CC, 3, n0 - 3, 8, PXR, 1)
        sweep(V if cyc == 0 else V3, WB, BB, CC, 4, n0 - 4, 8, PXR, 1)

    fl = halo_start(V3, SG0.at[4], RG0.at[4], H, own, PXR, X, hs=1)
    grown = 1.0 - KEEP ** 8

    @pl.loop(0, own)
    def _(a):
        for h in range(2):
            f = FL[h, 1 + a // 4, BASE:BASE + X]
            OST[0, h, a] = jnp.where(f > 0, V3[h, H + a, BASE:BASE + X], grown * FS[h, H + a, BASE:BASE + X])
    outs = [(remote(OST.at[0, other], p_out.at[pl.ds(p * own, own)], sib), None, None)]
    finish(fl)
    halo_place(V3, RG0.at[4], H, own, X, hs=1)

    @pl.loop(0, own)
    def _(a):
        r = remainder0(V3, H + a, KEEP ** 8)
        for h in range(2):
            OST[1, h, a] = r[h][H:H + X]
    outs.append((remote(OST.at[1, other], r_out.at[pl.ds(p * own, own)], sib), None, None))

    @pl.loop(0, own)
    def _(a):
        p_out[p * own + a] = OST[0, p, a]
        r_out[p * own + a] = OST[1, p, a]
    finish(outs)


def solution(mesh):
    ng = mesh.shape["azim"] * mesh.shape["pair"]
    nz = mesh.shape["axial"]

    def per_device(forcing, absorption, blocks):
        A, X, R = forcing.shape
        own = A // 2
        fl = jnp.repeat(jnp.repeat(blocks.astype(jnp.float32), 4, axis=1), 4, axis=2)
        px, p1 = X + 24, 48
        n0, n1 = own + 2 * H, own // 2 + 2 * H
        x2 = nz * (X // 4)
        n2, r2 = ng * 2, x2 + 16
        n3, r3 = ng, (x2 // 2 + 7) // 8 * 8 + 16
        V = lambda *s: pltpu.VMEM(s, jnp.float32)
        full = V(2, n0, px, 128)
        lev1 = V(2, n1, p1, 128)
        lev2 = V(2, n2, r2, 128)
        lev3 = V(2, n3, r3, 128)
        scratch = [
            V(own, X, 128), V(own, X, 128), V(own // 4, X, 128),
            full, full, V(2, own // 4 + 2, px, 128),
            full, full, full, full, full, full, full, V(8, 128), V(64, 128),
            V(5, 2, 2, own, H, 128), V(5, 2, 2, n0, H, 128),
            lev1, lev1, lev1, lev1, lev1, V(2, 2, n1, p1, 128), lev1, lev1,
            V(4, 2, 2, own // 2, H, 128), V(4, 2, 2, n1, H, 128),
            V(4, 16, 128), V(4, nz, 16, 128), V(4, ng, nz, 16, 128),
            lev2, lev2, lev2, lev2, lev2, lev2, lev2, lev2,
            V(2, own // 4 + 4, 16, 128), V(x2, 128), lev1, lev3, lev3, lev3, lev3,
            V(2, 2, own, X, 128),
            pltpu.SemaphoreType.DMA((SENDS,)), pltpu.SemaphoreType.DMA((SENDS,)),
        ]
        vm = pl.BlockSpec(memory_space=pltpu.VMEM)
        return pl.pallas_call(
            functools.partial(kernel, ng, nz, A, X),
            out_shape=[jax.ShapeDtypeStruct((A, X, R), jnp.float32)] * 2,
            in_specs=[vm] * 3, out_specs=[vm] * 2, scratch_shapes=scratch,
            compiler_params=pltpu.CompilerParams(
                collective_id=0, has_side_effects=True, vmem_limit_bytes=56 * 1024 * 1024),
        )(forcing, absorption, fl)

    spec = P("azim", "axial", "pair")
    return jax.shard_map(per_device, mesh=mesh, in_specs=(spec,) * 3, out_specs=(spec,) * 2, check_vma=False)
```

```python
import functools
import jax
import jax.numpy as jnp
from jax import lax
from jax.experimental import pallas as pl
from jax.experimental.pallas import tpu as pltpu
from jax.sharding import PartitionSpec as P

MESH = pl.DeviceIdType.MESH
H = 4
BASE = 12
DAMP = 0.8
KEEP = 0.2
SENDS = 136


def kernel(ng, nz, A, X, f_in, a_in, m_in, p_out, r_out,
           SWF, SWA, SWM, FS, AB, FL, DG, CC, BB, WA, WB, V, V3, RT, TMP,
           SG0, RG0, A1, F1, D1, C1, B1, S1, W1A, W1B, G1S, G1R,
           GL, GA, GB, D2, F2, A2, C2, S2, B2, W2A, W2B, LOC2, T2, AF, C3, B3, W3A, W3B,
           OST, send_sem, recv_sem):
    az, z, p = lax.axis_index("azim"), lax.axis_index("axial"), lax.axis_index("pair")
    g = az * 2 + p
    own = A // 2
    X1, X2L = X // 2, X // 4
    n2a, x2, n3a, x3 = ng * 2, nz * X2L, ng, nz * X2L // 2
    c3rows = (x3 + 7) // 8 * 8
    lane = lax.broadcasted_iota(jnp.int32, (1, 128), 1)
    counter = [0]

    def dev(gg, zz):
        return (gg // 2, zz, lax.rem(gg, 2))

    def gshift(o):
        return lax.rem(g + o + ng, ng)

    has_lo, has_hi = z > 0, z < nz - 1

    for ref in (WA, WB, AF, W1A, W1B, W2A, W2B, W3A, W3B, C3, B3):
        @pl.loop(0, ref.shape[1])
        def _(a, ref=ref):
            for h in range(2):
                ref[h, a] = jnp.zeros(ref.shape[2:], jnp.float32)
    for c in range(2):
        for h in range(2):
            S1[c, h] = jnp.zeros(S1.shape[2:], jnp.float32)
    bar = pltpu.get_barrier_semaphore()
    for o in range(1, ng):
        pl.semaphore_signal(bar, inc=1, device_id=dev(gshift(o), z), device_id_type=MESH)
    for o in range(1, nz):
        pl.semaphore_signal(bar, inc=1, device_id=dev(g, lax.rem(z + o, nz)), device_id_type=MESH)
    for cond, dz in ((has_lo, -1), (has_hi, 1)):
        @pl.when(cond)
        def _():
            for o in (-1, 1):
                pl.semaphore_signal(bar, inc=1, device_id=dev(gshift(o), z + dz), device_id_type=MESH)
    lows = jnp.where(has_lo, 2, 0) + jnp.where(has_hi, 2, 0)

    pl.semaphore_wait(bar, (ng - 1) + (nz - 1) + lows)

    def remote(src, dst, target, cond=None):
        k = counter[0]
        counter[0] += 1
        def make():
            return pltpu.make_async_remote_copy(
                src_ref=src, dst_ref=dst, send_sem=send_sem.at[k], recv_sem=recv_sem.at[k],
                device_id=target, device_id_type=MESH)
        if cond is None:
            make().start()
        else:
            pl.when(cond)(lambda: make().start())
        return make

    def finish(pairs):
        for make, cs, cr in pairs:
            if cs is None:
                make().wait_send()
                make().wait_recv()
            else:
                pl.when(cs)(lambda make=make: make().wait_send())
                pl.when(cr)(lambda make=make: make().wait_recv())

    def partner(y, s):
        return jnp.where((lane // s) % 2 == 0, pltpu.roll(y, 128 - s, 1), pltpu.roll(y, s, 1))

    def halo_start(buf, stg, rcv, ha, n, r0, nrows, hs=None):
        hs = ha if hs is None else hs
        last = BASE + nrows - H
        @pl.loop(0, n)
        def _(a):
            for h in range(2):
                stg[0, h, a] = buf[h, ha + a, BASE:BASE + H]
                stg[1, h, a] = buf[h, ha + a, last:last + H]
        end = r0
        out = []
        for o in (-1, 1):
            s0 = ha if o < 0 else ha + n - hs
            d0 = ha + n if o < 0 else ha - hs
            out.append((remote(buf.at[:, pl.ds(s0, hs), pl.ds(8, end)],
                               buf.at[:, pl.ds(d0, hs), pl.ds(8, end)],
                               dev(gshift(o), z)), None, None))
        for side, dz, cs, cr in ((0, -1, has_lo, has_hi), (1, 1, has_hi, has_lo)):
            for o in (-1, 0, 1):
                if o == 0:
                    src = stg.at[side]
                    dst = rcv.at[1 - side, :, pl.ds(ha, n)]
                else:
                    s0 = 0 if o < 0 else n - hs
                    d0 = ha + n if o < 0 else ha - hs
                    src = stg.at[side, :, pl.ds(s0, hs)]
                    dst = rcv.at[1 - side, :, pl.ds(d0, hs)]
                out.append((remote(src, dst, dev(gshift(o), z + dz), cs), cs, cr))
        return out

    def halo_place(buf, rcv, ha, n, nrows, hs=None):
        hs = ha if hs is None else hs
        for side, cond, row in ((0, has_lo, BASE - H), (1, has_hi, BASE + nrows)):
            @pl.when(cond)
            def _():
                @pl.loop(ha - hs, n + ha + hs)
                def _(a):
                    for h in range(2):
                        buf[h, a, row:row + H] = rcv[side, h, a]
            @pl.when(jnp.logical_not(cond))
            def _():
                @pl.loop(ha - hs, n + ha + hs)
                def _(a):
                    for h in range(2):
                        buf[h, a, row:row + H] = jnp.zeros((H, 128), jnp.float32)

    def beside(buf, a, up, dn, r0, n, s):
        cen = [buf[h, a, pl.ds(r0, n)] for h in range(2)]
        lf = [pltpu.roll(v, s, 1) for v in cen]
        rt = [pltpu.roll(v, 128 - s, 1) for v in cen]
        left = [jnp.where(lane < s, 0.0, lf[0]), jnp.where(lane < s, lf[0], lf[1])]
        right = [jnp.where(lane >= 128 - s, rt[1], rt[0]), jnp.where(lane >= 128 - s, 0.0, rt[1])]
        tot = []
        for h in range(2):
            t = buf[h, up, pl.ds(r0, n)] + buf[h, dn, pl.ds(r0, n)]
            t = t + buf[h, a, pl.ds(r0 + 1, n)] + buf[h, a, pl.ds(r0 - 1, n)]
            tot.append(t + left[h] + right[h])
        return cen, tot

    def sweep(dst, src, b, c, lo, hi, r0, n, s, ring=None, bidx=None):
        @pl.loop(lo, hi, unroll=4 if n > 40 else 8)
        def _(a):
            up, dn = (a + 1, a - 1) if ring is None else (lax.rem(a + 1, ring), lax.rem(a + ring - 1, ring))
            cen, tot = beside(src, a, up, dn, r0, n, s)
            for h in range(2):
                dst[h, a, pl.ds(r0, n)] = (KEEP * cen[h] + b[h, a, pl.ds(r0, n)]
                                           + c[h, a, pl.ds(r0, n)] * tot[h])

    other = 1 - p
    sib = (az, z, other)
    mo = own // 4
    sw = []
    for src, dst, n in ((f_in, SWF, own), (a_in, SWA, own), (m_in, SWM, mo)):
        sw.append((remote(src.at[pl.ds(other * n, n)], dst, sib), None, None))
    PXR = X + 2 * H
    P1R = 32

    for src, dst, n, ha in ((f_in, FS, own, H), (a_in, AB, own, H), (m_in, FL, mo, 1)):
        @pl.loop(0, n)
        def _(a, src=src, dst=dst, n=n, ha=ha):
            dst[p, ha + a, BASE:BASE + X] = src[p * n + a]
    finish(sw)
    for src, dst, n, ha in ((SWF, FS, own, H), (SWA, AB, own, H), (SWM, FL, mo, 1)):
        @pl.loop(0, n)
        def _(a, src=src, dst=dst, n=n, ha=ha):
            dst[other, ha + a, BASE:BASE + X] = src[a]

    flight = []
    stages = {}
    for i, (buf, ha, n) in enumerate(((FS, H, own), (AB, H, own), (FL, 1, mo))):
        flight += halo_start(buf, SG0.at[i, :, :, pl.ds(0, n)],
                             RG0.at[i, :, :, pl.ds(0, n + 2 * ha)], ha, n, PXR, X, hs=min(ha, H - 1))

    def rows2(n, r0, op):
        return op(TMP[pl.ds(r0, n, stride=2)], TMP[pl.ds(r0 + 1, n, stride=2)])

    @pl.loop(0, own // 2)
    def _(k):
        for h in range(2):
            TMP[0:PXR] = AB[h, H + 2 * k, 8:8 + PXR] + AB[h, H + 2 * k + 1, 8:8 + PXR]
            t = rows2(X1, BASE - 8, jnp.add)
            ab = 0.25 * (t + partner(t, 1))
            A1[h, H + k, BASE:BASE + X1] = ab
            TMP[0:PXR] = FL[h, 1 + k // 2, 8:8 + PXR]
            f = TMP[pl.ds(BASE - 8, X1, stride=2)]
            F1[h, H + k, BASE:BASE + X1] = f
            AF[h, H + k, BASE:BASE + X1] = jnp.where(lane % 2 == 0, ab, f)
    flight += halo_start(AF, G1S.at[0], G1R.at[0], H, own // 2, P1R, X1)

    def restrict2(buf, h, k, op):
        TMP[0:P1R] = op(buf[h, 2 * k, 8:8 + P1R], buf[h, 2 * k + 1, 8:8 + P1R])
        t = rows2(X2L, BASE - 8, op)
        return op(t, partner(t, 2))

    def put(slot, vals):
        y = jnp.where(lane % 4 == 0, vals[0], jnp.where(lane % 4 == 1, vals[1], jnp.where(lane % 4 == 2, vals[2], vals[3])))
        GL[slot, 0:X2L] = y

    def gather(slot, count):
        rs = []
        @pl.loop(0, count)
        def _(i):
            GA[slot + i, z] = GL[slot + i]
        for o in range(1, nz):
            rs.append((remote(GL.at[pl.ds(slot, count)], GA.at[pl.ds(slot, count), z],
                              dev(g, lax.rem(z + o, nz))), None, None))
        finish(rs)
        rs = []
        for o in range(1, ng):
            rs.append((remote(GA.at[pl.ds(slot, count)], GB.at[pl.ds(slot, count), g],
                              dev(gshift(o), z)), None, None))
        for i in range(count):
            for zz in range(nz):
                GB[slot + i, g, zz] = GA[slot + i, zz]
        finish(rs)

    def unpack(slot, dst):
        @pl.loop(0, ng)
        def _(gg):
            for zz in range(nz):
                t = GB[slot, gg, zz]
                for q in range(4):
                    y = jnp.where(lane % 4 == q, t, 0.0)
                    y = y + partner(y, 1)
                    y = y + partner(y, 2)
                    dst[q // 2, 2 * gg + q % 2, pl.ds(8 + X2L * zz, X2L)] = y[0:X2L]

    vals = [0.25 * restrict2(A1.at[:, pl.ds(H, own // 2)], q // 2, q % 2, jnp.add) for q in range(4)]
    put(0, vals)
    vals = [restrict2(F1.at[:, pl.ds(H, own // 2)], q // 2, q % 2, jnp.maximum) for q in range(4)]
    put(1, vals)
    gather(0, 2)
    unpack(0, A2)
    unpack(1, F2)

    R2 = x2
    @pl.loop(0, n2a)
    def _(a):
        for h in range(2):
            f = F2[h, a, pl.ds(8, R2)]
            d = f * (6.0 + A2[h, a, pl.ds(8, R2)]) + 1.0 - f
            D2[h, a, pl.ds(8, R2)] = d
            C2[h, a, pl.ds(8, R2)] = DAMP * f / d

    @pl.loop(0, n3a)
    def _(k):
        for h in range(2):
            T2[0:R2] = A2[h, 2 * k, pl.ds(8, R2)] + A2[h, 2 * k + 1, pl.ds(8, R2)]
            t = T2[pl.ds(0, x3, stride=2)] + T2[pl.ds(1, x3, stride=2)]
            ab = 0.25 * (t + partner(t, 4))
            T2[0:R2] = jnp.maximum(F2[h, 2 * k, pl.ds(8, R2)], F2[h, 2 * k + 1, pl.ds(8, R2)])
            t = jnp.maximum(T2[pl.ds(0, x3, stride=2)], T2[pl.ds(1, x3, stride=2)])
            f = jnp.maximum(t, partner(t, 4))
            C3[h, k, 8:8 + x3] = DAMP * f / (f * (6.0 + ab) + 1.0 - f)

    finish(flight)
    for i, (buf, ha, n) in enumerate(((FS, H, own), (AB, H, own), (FL, 1, mo))):
        halo_place(buf, RG0.at[i, :, :, pl.ds(0, n + 2 * ha)], ha, n, X, hs=min(ha, H - 1))
    halo_place(AF, G1R.at[0], H, own // 2, X1)

    @pl.loop(0, own + 2 * H)
    def _(a):
        for h in range(2):
            f = FL[h, a // 4, 8:8 + PXR]
            d = f * (6.0 + AB[h, a, 8:8 + PXR]) + 1.0 - f
            c = DAMP * f / d
            DG[h, a, 8:8 + PXR] = d
            CC[h, a, 8:8 + PXR] = c
            BB[h, a, 8:8 + PXR] = c * FS[h, a, 8:8 + PXR]

    @pl.loop(0, own // 2 + 2 * H)
    def _(a):
        for h in range(2):
            t = AF[h, a, 8:8 + P1R]
            swapped = partner(t, 1)
            f = jnp.where(lane % 2 == 0, swapped, t)
            F1[h, a, 8:8 + P1R] = f
            d = f * (6.0 + jnp.where(lane % 2 == 0, t, swapped)) + 1.0 - f
            D1[h, a, 8:8 + P1R] = d
            C1[h, a, 8:8 + P1R] = DAMP * f / d

    def remainder0(buf, a, solid):
        cen, tot = beside(buf, a, a + 1, a - 1, 8, PXR, 1)
        out = []
        for h in range(2):
            f = FL[h, a // 4, 8:8 + PXR]
            s = FS[h, a, 8:8 + PXR]
            out.append(jnp.where(f > 0, s - (DG[h, a, 8:8 + PXR] * cen[h] - tot[h]), solid * s))
        return out

    def level3():
        @pl.loop(0, n3a)
        def _(a):
            for h in range(2):
                W3A[h, a, pl.ds(8, c3rows)] = B3[h, a, pl.ds(8, c3rows)]
        for src, dst in ((W3A, W3B), (W3B, W3A), (W3A, W3B)):
            sweep(dst, src, B3, C3, 0, n3a, 8, c3rows, 8, ring=n3a)
        return W3B

    def level2():
        @pl.loop(0, n2a, unroll=4)
        def _(a):
            for h in range(2):
                b = C2[h, a, pl.ds(8, R2)] * S2[h, a, pl.ds(8, R2)]
                B2[h, a, pl.ds(8, R2)] = b
                W2A[h, a, pl.ds(8, R2)] = b
        sweep(W2B, W2A, B2, C2, 0, n2a, 8, R2, 4, ring=n2a)

        @pl.loop(0, n3a, unroll=4)
        def _(k):
            rem = [0.0, 0.0]
            for j in range(2):
                a = 2 * k + j
                cen, tot = beside(W2B, a, lax.rem(a + 1, n2a), lax.rem(a + n2a - 1, n2a), 8, R2, 4)
                for h in range(2):
                    s = S2[h, a, pl.ds(8, R2)]
                    rem[h] = rem[h] + jnp.where(F2[h, a, pl.ds(8, R2)] > 0,
                                                s - (D2[h, a, pl.ds(8, R2)] * cen[h] - tot[h]), (KEEP * KEEP) * s)
            for h in range(2):
                T2[0:R2] = rem[h]
                t = T2[pl.ds(0, x3, stride=2)] + T2[pl.ds(1, x3, stride=2)]
                B3[h, k, 8:8 + x3] = C3[h, k, 8:8 + x3] * (0.25 * (t + partner(t, 4)))
        w3 = level3()

        @pl.loop(0, n3a, unroll=4)
        def _(k):
            for h in range(2):
                v = w3[h, k, 8:8 + x3]
                T2[pl.ds(0, x3, stride=2)] = v
                T2[pl.ds(1, x3, stride=2)] = v
                t = T2[0:R2]
                for j in range(2):
                    W2A[h, 2 * k + j, pl.ds(8, R2)] = W2B[h, 2 * k + j, pl.ds(8, R2)] + F2[h, 2 * k + j, pl.ds(8, R2)] * t
        sweep(W2B, W2A, B2, C2, 0, n2a, 8, R2, 4, ring=n2a)
        sweep(W2A, W2B, B2, C2, 0, n2a, 8, R2, 4, ring=n2a)
        return W2A

    def level1(cyc):
        src = S1.at[cyc]
        fl = halo_start(src, G1S.at[2 + cyc], G1R.at[2 + cyc], H, own // 2, P1R, X1)
        finish(fl)
        halo_place(src, G1R.at[2 + cyc], H, own // 2, X1)
        n1 = own // 2 + 2 * H

        @pl.loop(0, n1)
        def _(a):
            for h in range(2):
                b = C1[h, a, 8:8 + P1R] * src[h, a, 8:8 + P1R]
                B1[h, a, 8:8 + P1R] = b
                W1A[h, a, 8:8 + P1R] = b
        sweep(W1B, W1A, B1, C1, 1, n1 - 1, 8, P1R, 2)

        vals = {}
        for k in range(2):
            rem = [0.0, 0.0]
            for j in range(2):
                a = H + 2 * k + j
                cen, tot = beside(W1B, a, a + 1, a - 1, 8, P1R, 2)
                for h in range(2):
                    s = src[h, a, 8:8 + P1R]
                    rem[h] = rem[h] + jnp.where(F1[h, a, 8:8 + P1R] > 0,
                                                s - (D1[h, a, 8:8 + P1R] * cen[h] - tot[h]), (KEEP * KEEP) * s)
            for h in range(2):
                TMP[0:P1R] = rem[h]
                t = rows2(X2L, BASE - 8, jnp.add)
                vals[(h, k)] = 0.25 * (t + partner(t, 2))
        put(2 + cyc, [vals[(q // 2, q % 2)] for q in range(4)])
        gather(2 + cyc, 1)
        unpack(2 + cyc, S2)
        w2 = level2()
        nl = own // 4 + 4
        for zz in range(nz):
            @pl.when(z == zz)
            def _(zz=zz):
                @pl.loop(0, nl)
                def _(j):
                    a = lax.rem(own // 4 * g + j - 2 + n2a, n2a)
                    for h in range(2):
                        LOC2[h, j, 0:16] = w2[h, a, 8 + X2L * zz - 2:8 + X2L * zz + 14]

        @pl.loop(0, nl)
        def _(j):
            for h in range(2):
                v = LOC2[h, j, 0:16]
                TMP[pl.ds(0, 16, stride=2)] = v
                TMP[pl.ds(1, 16, stride=2)] = v
                t = TMP[0:P1R]
                for i in range(2):
                    a = 2 * j + i
                    W1A[h, a, 8:8 + P1R] = W1B[h, a, 8:8 + P1R] + F1[h, a, 8:8 + P1R] * t
        sweep(W1B, W1A, B1, C1, 2, n1 - 2, 8, P1R, 2)
        sweep(W1A, W1B, B1, C1, 3, n1 - 3, 8, P1R, 2)
        return W1A

    n0 = own + 2 * H
    for cyc in range(2):
        if cyc == 0:
            sweep(WB, BB, BB, CC, 2, n0 - 2, 8, PXR, 1)
        else:
            fl = halo_start(V, SG0.at[3], RG0.at[3], H, own, PXR, X)
            finish(fl)
            halo_place(V, RG0.at[3], H, own, X)
            sweep(WA, V, BB, CC, 1, n0 - 1, 8, PXR, 1)
            sweep(WB, WA, BB, CC, 2, n0 - 2, 8, PXR, 1)
        solid = KEEP ** (2 if cyc == 0 else 6)

        @pl.loop(0, own // 2, unroll=2)
        def _(k):
            ra = remainder0(WB, H + 2 * k, solid)
            rb = remainder0(WB, H + 2 * k + 1, solid)
            for h in range(2):
                TMP[0:PXR] = ra[h] + rb[h]
                t = rows2(X1, BASE - 8, jnp.add)
                S1[cyc, h, H + k, BASE:BASE + X1] = 0.25 * (t + partner(t, 1))
        w1 = level1(cyc)

        @pl.loop(3, own // 2 + 2 * H - 3)
        def _(k):
            for h in range(2):
                v = w1[h, k, BASE - 2:BASE - 2 + X1 + 4]
                TMP[pl.ds(0, X1 + 4, stride=2)] = v
                TMP[pl.ds(1, X1 + 4, stride=2)] = v
                t = TMP[0:PXR]
                for i in range(2):
                    a = 2 * (k - 2) + i
                    WA[h, a, 8:8 + PXR] = WB[h, a, 8:8 + PXR] + jnp.where(FL[h, a // 4, 8:8 + PXR] > 0, t, 0.0)
        sweep(WB, WA, BB, CC, 3, n0 - 3, 8, PXR, 1)
        sweep(V if cyc == 0 else V3, WB, BB, CC, 4, n0 - 4, 8, PXR, 1)

    fl = halo_start(V3, SG0.at[4], RG0.at[4], H, own, PXR, X, hs=1)
    grown = 1.0 - KEEP ** 8

    @pl.loop(0, own)
    def _(a):
        for h in range(2):
            f = FL[h, 1 + a // 4, BASE:BASE + X]
            OST[0, h, a] = jnp.where(f > 0, V3[h, H + a, BASE:BASE + X], grown * FS[h, H + a, BASE:BASE + X])
    outs = [(remote(OST.at[0, other], p_out.at[pl.ds(p * own, own)], sib), None, None)]
    finish(fl)
    halo_place(V3, RG0.at[4], H, own, X, hs=1)

    @pl.loop(0, own)
    def _(a):
        r = remainder0(V3, H + a, KEEP ** 8)
        for h in range(2):
            OST[1, h, a] = r[h][H:H + X]
    outs.append((remote(OST.at[1, other], r_out.at[pl.ds(p * own, own)], sib), None, None))

    @pl.loop(0, own)
    def _(a):
        p_out[p * own + a] = OST[0, p, a]
        r_out[p * own + a] = OST[1, p, a]
    finish(outs)


def solution(mesh):
    ng = mesh.shape["azim"] * mesh.shape["pair"]
    nz = mesh.shape["axial"]

    def per_device(forcing, absorption, blocks):
        A, X, R = forcing.shape
        own = A // 2
        fl = jnp.repeat(jnp.repeat(blocks.astype(jnp.float32), 4, axis=1), 4, axis=2)
        px, p1 = X + 24, 48
        n0, n1 = own + 2 * H, own // 2 + 2 * H
        x2 = nz * (X // 4)
        n2, r2 = ng * 2, x2 + 16
        n3, r3 = ng, (x2 // 2 + 7) // 8 * 8 + 16
        V = lambda *s: pltpu.VMEM(s, jnp.float32)
        full = V(2, n0, px, 128)
        lev1 = V(2, n1, p1, 128)
        lev2 = V(2, n2, r2, 128)
        lev3 = V(2, n3, r3, 128)
        scratch = [
            V(own, X, 128), V(own, X, 128), V(own // 4, X, 128),
            full, full, V(2, own // 4 + 2, px, 128),
            full, full, full, full, full, full, full, V(8, 128), V(64, 128),
            V(5, 2, 2, own, H, 128), V(5, 2, 2, n0, H, 128),
            lev1, lev1, lev1, lev1, lev1, V(2, 2, n1, p1, 128), lev1, lev1,
            V(4, 2, 2, own // 2, H, 128), V(4, 2, 2, n1, H, 128),
            V(4, 16, 128), V(4, nz, 16, 128), V(4, ng, nz, 16, 128),
            lev2, lev2, lev2, lev2, lev2, lev2, lev2, lev2,
            V(2, own // 4 + 4, 16, 128), V(x2, 128), lev1, lev3, lev3, lev3, lev3,
            V(2, 2, own, X, 128),
            pltpu.SemaphoreType.DMA((SENDS,)), pltpu.SemaphoreType.DMA((SENDS,)),
        ]
        vm = pl.BlockSpec(memory_space=pltpu.VMEM)
        return pl.pallas_call(
            functools.partial(kernel, ng, nz, A, X),
            out_shape=[jax.ShapeDtypeStruct((A, X, R), jnp.float32)] * 2,
            in_specs=[vm] * 3, out_specs=[vm] * 2, scratch_shapes=scratch,
            compiler_params=pltpu.CompilerParams(
                collective_id=0, has_side_effects=True, vmem_limit_bytes=56 * 1024 * 1024),
        )(forcing, absorption, fl)

    spec = P("azim", "axial", "pair")
    return jax.shard_map(per_device, mesh=mesh, in_specs=(spec,) * 3, out_specs=(spec,) * 2, check_vma=False)
```
